32 devices in a mesh: span: 16 (over z, x, core), chord: 2 (over y).
Axes of the slice: x: 2, y: 2, z: 4, core: 2. Of those that a mesh axis runs over, the one named last changes fastest.
Arguments:
- adjoint_flow: float32 [5, 16, 128, 256], P(None, None, 'span', 'chord'), may hold values from -6 to 6
- flow_grad: float32 [5, 16, 128, 256], P(None, None, 'span', 'chord'), may hold values from -6 to 6
- diagonal: float32 [16, 128, 256], P(None, 'span', 'chord'), may hold values from 4 to 6
- couplings: float32 [3, 16, 128, 256], P(None, None, 'span', 'chord'), may hold values from 0.3 to 1.5
- upwind: float32 [3, 5, 5], replicated, may hold values from -2.5 to 2.5
- downwind: float32 [3, 5, 5], replicated, may hold values from -2.5 to 2.5
- pressure_row: float32 [5], replicated, may hold values from -4 to 4
- face_normal: float32 [3, 128, 256], P(None, 'span', 'chord'), may hold values from -6 to 6
- face_node: int32 [128, 256], P('span', 'chord'), may hold values from 0 to 16383, as said below
- face_count: int32 [16, 2], P('span', 'chord'), may hold values from 128 to 1024, as said below
- adjoint_shell: float32 [6, 16384], P(None, 'span'), may hold values from -6 to 6
- shell_grad: float32 [6, 16384], P(None, 'span'), may hold values from -6 to 6
- node_precond: float32 [6, 6, 16384], P(None, None, 'span'), as said below
- element_stiffness: float32 [24, 24, 4096], P(None, None, ('span', 'chord')), as said below
- connectivity: int32 [4, 4096], P(None, ('span', 'chord')), may hold values from 0 to 16383, as said below
Outputs:
- flow_adjoint: float32 [5, 16, 128, 256], P(None, None, 'span', 'chord')
- shell_adjoint: float32 [6, 16384], P(None, 'span')
The draws below stay inside these ranges and needn't reach their ends.
Inputs may be any that keep to these rules, and one draw needn't show every extreme that they name: `face_node`: a wall face in the span cells of span index s names a node from max(s - 1, 0) * 1024 to min(s + 2, 16) * 1024 - 1. `face_count`: on each device the wall faces in use are the first ones in span-major, chord-minor order. `connectivity`: the elements of span index s use nodes from s * 1024 to min((s + 1) * 1024 + 64, 16384) - 1. `node_precond`: each node block is near 0.15 times the identity. `element_stiffness`: each element block is symmetric and near the identity.
All inputs are finite; a program needn't handle non-finite values.
Results may differ from the reference program's by a relative error of at most 0.00013.
Values sent between devices are 32-bit elements; how exact they have to be, the bound alone decides.
A program may use at most 64 MiB of HBM per device.

```python
import math
import jax
import jax.numpy as jnp
from jax import lax

CN = 16
CS = 8
CC = 128
NODE_DEV = 1024
ELEM_DEV = 128
NB = 64
SW = 4
SS = 3
NS = 128
NC = 256
NODES = 16384
ELEMS = 4096
WALLF = 1024


def draw_face_node(key, part):
    span_rows = jnp.arange(NS, dtype=jnp.int32)[:, None]
    owner = span_rows // CS
    lower = jnp.maximum(owner - 1, 0) * NODE_DEV
    upper = jnp.minimum(owner + 2, NS // CS) * NODE_DEV
    raw_bits = jax.random.randint(key, (NS, NC), 0, 1 << 24)
    nodes = lower + raw_bits % (upper - lower)
    leading = span_rows % CS == 0
    local_chord = jnp.arange(NC, dtype=jnp.int32)[None, :] % CC
    nodes = jnp.where(leading & (local_chord == 0), lower, nodes)
    nodes = jnp.where(leading & (local_chord == 1), upper - 1, nodes)
    return nodes.astype(jnp.int32)


def draw_face_count(key, part):
    spans = NS // CS
    chords = NC // CC
    counts = jax.random.randint(key, (spans, chords), WALLF // 8, WALLF + 1)
    picked = jax.random.randint(jax.random.fold_in(key, 11), (spans, 1), 0, chords)
    chord_ids = jnp.arange(chords, dtype=jnp.int32)[None, :]
    counts = jnp.where(chord_ids == picked, WALLF, counts)
    counts = jnp.where(chord_ids == (picked + 1) % chords, WALLF // 8, counts)
    return counts.astype(jnp.int32)


def draw_connectivity(key, part):
    owners = NODES // NODE_DEV
    element = jnp.arange(ELEMS, dtype=jnp.int32)[None, :]
    owner = element // (ELEMS // owners)
    lower = owner * NODE_DEV
    upper = jnp.minimum(lower + NODE_DEV + NB, NODES)
    raw_bits = jax.random.randint(key, (4, ELEMS), 0, 1 << 24)
    nodes = lower + raw_bits % (upper - lower)
    leading = element % ELEM_DEV == 0
    corner = jnp.arange(4, dtype=jnp.int32)[:, None]
    nodes = jnp.where(leading & (corner == 0), lower, nodes)
    nodes = jnp.where(leading & (corner == 1), upper - 1, nodes)
    return nodes.astype(jnp.int32)


def draw_element_stiffness(key, part):
    noise = jax.random.normal(key, (24, 24, ELEMS), jnp.float32)
    symmetric = 0.5 * (noise + jnp.transpose(noise, (1, 0, 2)))
    identity = jnp.eye(24, dtype=jnp.float32)[:, :, None]
    return (identity + 0.06 * symmetric).astype(jnp.float32)


def draw_node_precond(key, part):
    noise = jax.random.normal(key, (6, 6, NODES), jnp.float32)
    identity = jnp.eye(6, dtype=jnp.float32)[:, :, None]
    return (0.15 * identity + 0.02 * noise).astype(jnp.float32)


def block_scale(stream_key, shape, pieces, low, high):
    def one(position, shards_of):
        draws = jax.random.uniform(jax.random.fold_in(jax.random.fold_in(stream_key, 6), position), (shards_of,), jnp.float32, low / len(pieces), high / len(pieces))
        return jnp.repeat(jnp.exp(draws), shape[position] // shards_of).reshape((-1,) + (1,) * (len(shape) - position - 1))

    level = one(*pieces[0])
    for cut in pieces[1:]:
        level = level * one(*cut)
    return level


def gaussian(key, dims, scale, most, shards=(), kind=jnp.bfloat16):
    entries = jax.random.normal(key, dims, jnp.float32) * scale
    if len(shards) > 0:
        entries = block_scale(key, dims, shards, -0.22, 0.18) * entries
    return jnp.clip(entries, min=-most, max=most).astype(kind)


def setup_inputs(seed: int = 0) -> dict:
    keys = jax.random.split(jax.random.key(seed), 16)
    return {
        "adjoint_flow": gaussian(keys[0], (5, CN, NS, NC), 1.0, 6.0, ((2, 16), (3, 2)), jnp.float32),
        "flow_grad": gaussian(keys[1], (5, CN, NS, NC), 1.0, 6.0, ((2, 16), (3, 2)), jnp.float32),
        "diagonal": jnp.clip(4.0 + 2.0 * jax.random.uniform(keys[2], (CN, NS, NC), jnp.float32) ** block_scale(keys[2], (CN, NS, NC), ((1, 16), (2, 2)), -0.2, 0.2), 4.0, 6.0),
        "couplings": jnp.clip(jnp.exp(math.log(1.5) - 1.60943787 * jax.random.uniform(keys[3], (3, CN, NS, NC), jnp.float32) ** block_scale(keys[3], (3, CN, NS, NC), ((2, 16), (3, 2)), -0.2, 0.2)), 0.3, 1.5),
        "upwind": gaussian(keys[4], (3, 5, 5), 5 ** -0.5, 2.5, (), jnp.float32),
        "downwind": gaussian(keys[5], (3, 5, 5), 5 ** -0.5, 2.5, (), jnp.float32),
        "pressure_row": gaussian(keys[6], (5,), 1.0, 4.0, (), jnp.float32),
        "face_normal": gaussian(keys[7], (3, NS, NC), 1.0, 6.0, ((1, 16), (2, 2)), jnp.float32),
        "face_node": draw_face_node(jax.random.fold_in(keys[15], 71), 0),
        "face_count": draw_face_count(jax.random.fold_in(keys[15], 71), 0),
        "adjoint_shell": gaussian(keys[10], (6, NODES), 1.0, 6.0, ((1, 16),), jnp.float32),
        "shell_grad": gaussian(keys[11], (6, NODES), 1.0, 6.0, ((1, 16),), jnp.float32),
        "node_precond": draw_node_precond(jax.random.fold_in(keys[15], 71), 0),
        "element_stiffness": draw_element_stiffness(jax.random.fold_in(keys[15], 71), 0),
        "connectivity": draw_connectivity(jax.random.fold_in(keys[15], 71), 0),
    }


def relax_cells(state, inv_diag, couplings, source, upwind, downwind):
    centre = state[:, :, 1:-1, 1:-1]
    normal_pad = jnp.pad(centre, ((0, 0), (1, 1), (0, 0), (0, 0)))
    pairs = ((normal_pad[:, 2:], normal_pad[:, :-2]),
             (state[:, :, 2:, 1:-1], state[:, :, :-2, 1:-1]),
             (state[:, :, 1:-1, 2:], state[:, :, 1:-1, :-2]))
    neighbours = jnp.zeros_like(source)
    for direction in range(3):
        forward, backward = pairs[direction]
        flux_term = jnp.einsum("ij,jnsc->insc", upwind[direction], forward, precision=lax.Precision.HIGHEST)
        flux_term = flux_term + jnp.einsum("ij,jnsc->insc", downwind[direction], backward, precision=lax.Precision.HIGHEST)
        neighbours = neighbours + couplings[direction][None] * flux_term
    return inv_diag[None] * (source + neighbours)


def stiffness(field, element_stiffness, connectivity):
    count_elems = connectivity.shape[1]
    element_values = field[:, connectivity]
    element_values = jnp.transpose(element_values, (1, 0, 2)).reshape(24, count_elems)
    element_forces = jnp.einsum("ije,je->ie", element_stiffness, element_values, precision=lax.Precision.HIGHEST)
    element_forces = jnp.transpose(element_forces.reshape(4, 6, count_elems), (1, 0, 2)).reshape(6, 4 * count_elems)
    return jax.ops.segment_sum(element_forces.T, connectivity.reshape(-1), field.shape[1]).T


def reference(adjoint_flow, flow_grad, diagonal, couplings, upwind, downwind, pressure_row, face_normal, face_node, face_count, adjoint_shell, shell_grad, node_precond, element_stiffness, connectivity):
    wall_layer = adjoint_flow[:, 0]
    span_index = jnp.arange(NS, dtype=jnp.int32)[:, None]
    chord_index = jnp.arange(NC, dtype=jnp.int32)[None, :]
    local_index = (span_index % CS) * CC + chord_index % CC
    counts = face_count[span_index // CS, chord_index // CC]
    active = (local_index < counts).astype(jnp.float32)
    pressure = jnp.einsum("j,jsc->sc", pressure_row, wall_layer, precision=lax.Precision.HIGHEST) * active
    loads_face = face_normal * pressure[None]
    node_load = jax.ops.segment_sum(loads_face.reshape(3, -1).T, face_node.reshape(-1), NODES).T
    load_full = jnp.concatenate([node_load, jnp.zeros((3, NODES), jnp.float32)], axis=0)
    shell_state = adjoint_shell
    for turn_index in range(SS):
        residual = shell_grad - load_full - stiffness(shell_state, element_stiffness, connectivity)
        shell_state = shell_state + jnp.einsum("ijn,jn->in", node_precond, residual, precision=lax.Precision.HIGHEST)
    picked = shell_state[:3][:, face_node]
    disp = jnp.einsum("isc,isc->sc", face_normal, picked, precision=lax.Precision.HIGHEST) * active
    source = flow_grad.at[:, 0].add(-pressure_row[:, None, None] * disp[None])
    inv_diag = 1.0 / diagonal
    state = adjoint_flow
    for turn_index in range(SW):
        padded = jnp.pad(state, ((0, 0), (0, 0), (1, 1), (1, 1)))
        state = relax_cells(padded, inv_diag, couplings, source, upwind, downwind)
    return state, shell_state
```

```python
import functools

import jax
import jax.numpy as jnp
from jax import lax
from jax.experimental import pallas as pl
from jax.experimental.pallas import tpu as pltpu
from jax.sharding import PartitionSpec as P

SW = 4
SS = 3
LANES = 128
ROWS = 8
DEPTH = 3
MESH = pl.DeviceIdType.MESH
F32 = jnp.float32
BF16 = jnp.bfloat16


def split(x):
    lead = x.astype(BF16).astype(F32)
    return jnp.concatenate([lead, x - lead], axis=0).astype(BF16)


def halves(x):
    rows = x.shape[0] // 2
    return x[:rows] + x[rows:]


def dot_nn(a, b):
    return lax.dot_general(a, b, (((1,), (0,)), ((), ())), preferred_element_type=F32)


def dot_nt(a, b):
    return lax.dot_general(a, b, (((1,), (1,)), ((), ())), preferred_element_type=F32)


def flat(tile):
    return jnp.concatenate([tile[r : r + 1] for r in range(tile.shape[0])], axis=1)


def one_hot_lanes(low):
    rows = lax.broadcasted_iota(jnp.int32, (LANES, low.shape[1]), 0)
    return jnp.where(rows == low, 1.0, 0.0).astype(BF16)


def kernel(
    spans, chords, flow, fgrad, diag, coup, upw, dnw, prow, fnorm, fnode, fcount,
    shell0, sgrad, precond, stiff, conn, flow_out, shell_out,
    state, top_s, bot_s, lft_s, rgt_s, top_r, bot_r, lft_r, rgt_r,
    rim_s, rim_r, pt, ptrim, load_s, load_own, load_up, load_dn,
    face_s, face_r, ext_s, ext_r, kv, kv_prev, kv_next, rhs_s, rhs_r,
    ct, ct_r, hot_face, hot_elem, weight, send_sem, recv_sem,
):
    s = lax.axis_index("span")
    c = lax.axis_index("chord")
    layers = flow.shape[1]
    node_dev = shell0.shape[1]
    chunks = node_dev // LANES
    own_rows = ROWS * chunks
    has = {-1: s >= 1, 1: s < spans - 1, -2: s >= 2, 2: s < spans - 2, 0: None}
    hasc = {-1: c >= 1, 1: c < chords - 1, 0: None}

    def both(a, b):
        if a is None:
            return b
        return a if b is None else jnp.logical_and(a, b)

    def when(cond, run):
        if cond is None:
            run()
        else:
            pl.when(cond)(run)

    def mask(cond, x):
        return x if cond is None else jnp.where(cond, x, 0.0)

    barrier = pltpu.get_barrier_semaphore()
    expected = jnp.int32(0)
    for ds in range(-2, 3):
        for k in range(chords):
            if ds == 0 and k == 0:
                continue
            target = (s + ds, lax.rem(c + k, chords))
            when(
                has[ds],
                lambda target=target: pl.semaphore_signal(
                    barrier, inc=1, device_id=target, device_id_type=MESH
                ),
            )
            expected += 1 if ds == 0 else has[ds].astype(jnp.int32)

    ends = []
    used = [0]

    def transfer(src, dst, landing, target, goes, comes):
        i = used[0]
        used[0] += 1

        def make(where):
            return pltpu.make_async_remote_copy(
                src_ref=src, dst_ref=where, send_sem=send_sem.at[i],
                recv_sem=recv_sem.at[i], device_id=target, device_id_type=MESH,
            )

        when(goes, lambda: make(dst).start())
        ends.append(lambda: when(goes, lambda: make(dst).wait_send()))
        return lambda: when(comes, lambda: make(landing).wait_recv())

    def to_span(src, dst, ds):
        return transfer(src, dst, dst, (s + ds, c), has[ds], has[-ds])

    def to_chord(src, dst, dc):
        return transfer(src, dst, dst, (s, c + dc), hasc[dc], hasc[-dc])

    def to_all(src, buf, ds):
        out = []
        for k in range(1 if ds == 0 else 0, chords):
            target = (s + ds, lax.rem(c + k, chords))
            origin = lax.rem(c - k + chords, chords)
            out.append(
                transfer(src, buf.at[c], buf.at[origin], target, has[ds], has[-ds])
            )
        return out

    row = lax.broadcasted_iota(jnp.int32, (ROWS, LANES), 0)
    lane = lax.broadcasted_iota(jnp.int32, (ROWS, LANES), 1)
    zero = jnp.zeros((ROWS, LANES), F32)
    pad2 = jnp.zeros((2, LANES), F32)

    def chunk(ref, h):
        return jnp.concatenate([ref[:, h * LANES : (h + 1) * LANES], pad2], axis=0)

    field = jnp.concatenate([chunk(shell0, h) for h in range(chunks)], axis=0)
    rim_s[...] = field[:ROWS]

    def pack(tile, n, k, j, left, right):
        top_s[k, j, pl.ds(n, 1), :] = tile[0:1]
        bot_s[k, j, pl.ds(n, 1), :] = tile[ROWS - 1 : ROWS]
        left = jnp.where(lane == n, pltpu.roll(tile, n, 1), left)
        right = jnp.where(lane == n, pltpu.roll(tile, n + 1, 1), right)
        return left, right

    def store_packs(k, packs):
        for j in range(5):
            lft_s[k, j] = packs[2 * j]
            rgt_s[k, j] = packs[2 * j + 1]

    def first_edges(n, packs):
        out = []
        for j in range(5):
            out += pack(flow[j, n], n, 0, j, packs[2 * j], packs[2 * j + 1])
        return tuple(out)

    store_packs(0, lax.fori_loop(0, layers, first_edges, (zero,) * 10))

    pl.semaphore_wait(barrier, expected)

    rim_came = to_span(rim_s, rim_r, -1)

    def send_edges(k):
        return [
            to_span(top_s.at[k], top_r.at[k], -1),
            to_span(bot_s.at[k], bot_r.at[k], 1),
            to_chord(lft_s.at[k], lft_r.at[k], -1),
            to_chord(rgt_s.at[k], rgt_r.at[k], 1),
        ]

    edges_came = send_edges(0)

    active = jnp.where(row * LANES + lane < fcount[0, 0], 1.0, 0.0)
    press = prow[0] * flow[0, 0]
    for j in range(1, 5):
        press = press + prow[j] * flow[j, 0]
    press = press * active
    nodes = flat(fnode[...])
    hot_face[1] = one_hot_lanes(jnp.bitwise_and(nodes, LANES - 1))
    own_chunk = jnp.right_shift(nodes - s * node_dev, 7)
    faces = nodes.shape[1]
    rows_f = lax.broadcasted_iota(jnp.int32, (chunks, faces), 0)
    loads = [flat(fnorm[i] * press) for i in range(3)]
    spread = []
    for owner in range(-1, 2):
        here = rows_f + owner * chunks == own_chunk
        for i in range(3):
            spread.append(jnp.where(here, loads[i], 0.0))
    partial = halves(dot_nt(split(jnp.concatenate(spread, axis=0)), hot_face[1]))
    third = 3 * chunks
    for o in range(3):
        load_s[o] = partial[o * third : (o + 1) * third]
    load_own[c] = partial[third : 2 * third]
    loads_came = to_all(load_s.at[1], load_own, 0)
    loads_came += to_all(load_s.at[2], load_up, 1)
    loads_came += to_all(load_s.at[0], load_dn, -1)

    local = conn[...] - s * node_dev
    enode = flat(local)
    echunk = jnp.right_shift(enode, 7)
    hot_elem[...] = one_hot_lanes(jnp.bitwise_and(enode, LANES - 1))
    elems = conn.shape[1]

    def stiffness(field, rim, r):
        table = jnp.concatenate([field, rim], axis=0)
        got = halves(dot_nn(split(table), hot_elem[...]))
        u = jnp.where(echunk == 0, got[:ROWS], 0.0)
        for h in range(1, chunks + 1):
            u = jnp.where(echunk == h, got[h * ROWS : (h + 1) * ROWS], u)
        parts = [None] * 4
        for a in range(4):
            for d in range(6):
                term = stiff[6 * a + d] * u[d : d + 1, a * elems : (a + 1) * elems]
                parts[a] = term if parts[a] is None else parts[a] + term
        f = (parts[0] + parts[1]) + (parts[2] + parts[3])
        force = jnp.concatenate(
            [jnp.concatenate([f[6 * a : 6 * a + 6], pad2], axis=0) for a in range(4)], axis=1
        )
        spread = jnp.concatenate(
            [jnp.where(echunk == h, force, 0.0) for h in range(chunks + 1)], axis=0
        )
        kv[r, c] = halves(dot_nt(split(spread), hot_elem[...]))
        came = to_all(kv.at[r, c], kv.at[r], 0)
        came += to_all(kv.at[r, c, pl.ds(own_rows, ROWS)], kv_prev.at[r], 1)
        if r < SS - 1:
            came += to_all(kv.at[r, c, pl.ds(0, ROWS)], kv_next.at[r], -1)
        return came

    rim_came()
    rim = mask(has[1], rim_r[...])
    kv_came = stiffness(field, rim, 0)

    for d2 in range(6):
        col = jnp.concatenate(
            [precond[d, d2 : d2 + 1, :] for d in range(6)] + [jnp.zeros((2, node_dev), F32)], axis=0
        )
        for h in range(chunks):
            pt[h, d2] = col[:, h * LANES : (h + 1) * LANES]
    pt_came = to_span(pt.at[0], ptrim, -1)

    def total(buf):
        t = buf[0]
        for k in range(1, chords):
            t = t + buf[k]
        return t

    for came in loads_came:
        came()
    load = total(load_own) + mask(has[-1], total(load_up)) + mask(has[1], total(load_dn))
    rhs_rows = []
    for h in range(chunks):
        part = jnp.concatenate(
            [load[i * chunks + h : i * chunks + h + 1] for i in range(3)]
            + [jnp.zeros((ROWS - 3, LANES), F32)], axis=0,
        )
        rhs_rows.append(chunk(sgrad, h) - part)
    rhs = jnp.concatenate(rhs_rows, axis=0)
    rhs_s[...] = rhs[:ROWS]
    rhs_came = to_span(rhs_s, rhs_r, -1)

    node_f = fnode[...].astype(F32)
    for i in range(3):
        face_s[i] = fnorm[i] * active
    face_s[3] = node_f
    faces_came = [to_span(face_s, face_r.at[0], 1), to_span(face_s, face_r.at[1], -1)]
    for n in range(DEPTH):
        for k in range(3):
            ext_s[3 * n + k] = coup[k, n]
        ext_s[3 * DEPTH + n] = 1.0 / diag[n]
    ext_came = []
    for a in range(-1, 2):
        for b in range(-1, 2):
            if a == 0 and b == 0:
                continue
            slot = ext_r.at[a + 1, b + 1]
            ext_came.append(
                transfer(
                    ext_s, slot, slot, (s - a, c - b),
                    both(has[-a], hasc[-b]), both(has[a], hasc[b]),
                )
            )

    def mix(mat, k, tiles):
        out = []
        for i in range(5):
            t = mat[k, i, 0] * tiles[0]
            for j in range(1, 5):
                t = t + mat[k, i, j] * tiles[j]
            out.append(t)
        return out

    def flow_sweep(k, src, dst, came):
        for wait in came:
            wait()

        def body(n, packs):
            above, below = jnp.minimum(n + 1, layers - 1), jnp.maximum(n - 1, 0)
            inv = 1.0 / diag[n]
            acc = [fgrad[j, n] for j in range(5)]
            cur = [src(j, n) for j in range(5)]
            nxt = [jnp.where(n < layers - 1, src(j, above), 0.0) for j in range(5)]
            prv = [jnp.where(n > 0, src(j, below), 0.0) for j in range(5)]
            for d in range(3):
                if d == 0:
                    fwd, bwd = nxt, prv
                elif d == 1:
                    fwd, bwd = [], []
                    for j in range(5):
                        down = mask(has[1], top_r[k, j, pl.ds(n, 1), :])
                        up = mask(has[-1], bot_r[k, j, pl.ds(n, 1), :])
                        fwd.append(jnp.where(row == ROWS - 1, down, pltpu.roll(cur[j], ROWS - 1, 0)))
                        bwd.append(jnp.where(row == 0, up, pltpu.roll(cur[j], 1, 0)))
                else:
                    fwd, bwd = [], []
                    for j in range(5):
                        right = mask(hasc[1], pltpu.roll(lft_r[k, j], LANES - 1 - n, 1))
                        left = mask(hasc[-1], pltpu.roll(rgt_r[k, j], LANES - n, 1))
                        fwd.append(jnp.where(lane == LANES - 1, right, pltpu.roll(cur[j], LANES - 1, 1)))
                        bwd.append(jnp.where(lane == 0, left, pltpu.roll(cur[j], 1, 1)))
                one, two = mix(upw, d, fwd), mix(dnw, d, bwd)
                w = coup[d, n]
                acc = [acc[i] + w * (one[i] + two[i]) for i in range(5)]
            out = []
            for j in range(5):
                tile = inv * acc[j]
                dst(j, n, tile)
                if k < SW - 1:
                    out += pack(tile, n, k + 1, j, packs[2 * j], packs[2 * j + 1])
            return tuple(out)

        packs = lax.fori_loop(0, layers, body, (zero,) * 10 if k < SW - 1 else ())
        if k < SW - 1:
            store_packs(k + 1, packs)
            return send_edges(k + 1)
        return []

    def from_input(j, n):
        return flow[j, n]

    def reader(b):
        return lambda j, n: state[b, j, n]

    def writer(b):
        def put(j, n, tile):
            state[b, j, n] = tile

        return put

    def apply(blocks, res):
        out = blocks(0) * res[0:1]
        for d in range(1, 6):
            out = out + blocks(d) * res[d : d + 1]
        return out

    for r in range(SS):
        edges_came = flow_sweep(
            r, from_input if r == 0 else reader((r + 1) % 2), writer(r % 2), edges_came
        )
        if r == 0:
            for wait in faces_came:
                wait()
            for t in (-1, 0, 1):
                if t == 0:
                    tnodes, normals = nodes, [flat(face_s[i]) for i in range(3)]
                else:
                    got = face_r.at[0 if t == -1 else 1]
                    raw = mask(has[t], got[3]).astype(jnp.int32)
                    tnodes = flat(raw)
                    normals = [flat(mask(has[t], got[i])) for i in range(3)]
                    hot_face[t + 1] = one_hot_lanes(jnp.bitwise_and(tnodes, LANES - 1))
                here = rows_f == jnp.right_shift(tnodes - s * node_dev, 7)
                for i in range(3):
                    weight[t + 1, i] = jnp.where(here, normals[i], 0.0)
            pt_came()
            rhs_came()
            rhs_rim = mask(has[1], rhs_r[...])
        for wait in kv_came:
            wait()
        own = kv[r, 0, pl.ds(0, own_rows), :]
        for k in range(1, chords):
            own = own + kv[r, k, pl.ds(0, own_rows), :]
        spill = mask(has[-1], total(kv_prev.at[r]))
        res = rhs - jnp.concatenate([own[:ROWS] + spill, own[ROWS:]], axis=0)
        if r < SS - 1:
            mine = kv[r, 0, pl.ds(own_rows, ROWS), :]
            for k in range(1, chords):
                mine = mine + kv[r, k, pl.ds(own_rows, ROWS), :]
            res_rim = rhs_rim - (mask(has[1], total(kv_next.at[r])) + mine)
            rim = rim + mask(has[1], apply(lambda d: ptrim[d], res_rim))
        field = field + jnp.concatenate(
            [
                apply(lambda d, h=h: pt[h, d], res[h * ROWS : (h + 1) * ROWS])
                for h in range(chunks)
            ],
            axis=0,
        )
        if r < SS - 1:
            kv_came = stiffness(field, rim, r + 1)

    by_comp = jnp.concatenate(
        [field[h * ROWS + i : h * ROWS + i + 1] for i in range(3) for h in range(chunks)], axis=0
    )
    two = split(by_comp)
    for t in range(3):
        got = halves(dot_nn(two, hot_face[t]))
        acc = weight[t, 0] * got[:chunks]
        for i in range(1, 3):
            acc = acc + weight[t, i] * got[i * chunks : (i + 1) * chunks]
        share = jnp.sum(acc, axis=0, keepdims=True)
        ct[t] = jnp.concatenate(
            [share[:, r * LANES : (r + 1) * LANES] for r in range(ROWS)], axis=0
        )
    ct_came = []
    for ds in range(-2, 3):
        low, high = max(-1, ds - 1) + 1, min(1, ds + 1) + 2
        for dc in range(-1, 2):
            if ds == 0 and dc == 0:
                continue
            piece = pl.ds(low, high - low)
            slot = ct_r.at[2 - ds, 1 - dc, piece]
            ct_came.append(
                transfer(
                    ct.at[piece], slot, slot, (s + ds, c + dc),
                    both(has[ds], hasc[dc]), both(has[-ds], hasc[-dc]),
                )
            )
    for h in range(chunks):
        shell_out[:, h * LANES : (h + 1) * LANES] = field[h * ROWS : h * ROWS + 6]

    def put_out(j, n, tile):
        flow_out[j, n] = tile

    flow_sweep(SW - 1, reader((SW - 2) % 2), put_out, edges_came)

    for wait in ext_came:
        wait()

    def extended(get):
        def at(a, b):
            return get(a, b) if a == 0 and b == 0 else mask(both(has[a], hasc[b]), get(a, b))

        def sides(a):
            return jnp.where(lane < LANES // 2, at(a, 1), at(a, -1))

        upper = jnp.concatenate([at(0, 0), sides(0)], axis=1)
        span_halo = jnp.where(row < ROWS // 2, at(1, 0), at(-1, 0))
        corner = jnp.where(row < ROWS // 2, sides(1), sides(-1))
        return jnp.concatenate([upper, jnp.concatenate([span_halo, corner], axis=1)], axis=0)

    def ext_of(q):
        return extended(lambda a, b: ext_s[q] if a == 0 and b == 0 else ext_r[a + 1, b + 1, q])

    cext = [[ext_of(3 * n + k) for k in range(3)] for n in range(DEPTH)]
    iext = [ext_of(3 * DEPTH + n) for n in range(DEPTH)]

    for wait in ct_came:
        wait()

    def disp_at(tau, dc):
        out = None
        for t in range(-1, 2):
            sigma = tau - t
            if sigma == 0 and dc == 0:
                part = ct[t + 1]
            else:
                part = mask(both(has[sigma], hasc[dc]), ct_r[sigma + 2, dc + 1, t + 1])
            out = part if out is None else out + part
        return out

    disp = extended(disp_at)
    dsrc = [-prow[j] * disp for j in range(5)]

    def crop(x):
        return x[:ROWS, :LANES]

    def add(a, b):
        return b if a is None else [x + y for x, y in zip(a, b)]

    delta = [[iext[0] * dsrc[j] for j in range(5)]]
    for turn in range(1, SW):
        last = turn == SW - 1
        cut = crop if last else (lambda x: x)
        new = []
        for n in range(turn + 1):
            acc = [cut(x) for x in dsrc] if n == 0 else None
            if n < DEPTH:
                cs, inv = [cut(x) for x in cext[n]], cut(iext[n])
            else:
                cs, inv = [coup[k, n] for k in range(3)], 1.0 / diag[n]
            normal = None
            if n + 1 < len(delta):
                normal = mix(upw, 0, [cut(x) for x in delta[n + 1]])
            if n >= 1:
                normal = add(normal, mix(dnw, 0, [cut(x) for x in delta[n - 1]]))
            if normal is not None:
                acc = add(acc, [cs[0] * x for x in normal])
            if n < len(delta):
                here = delta[n]
                for d, axis, size in ((1, 0, 2 * ROWS), (2, 1, 2 * LANES)):
                    fwd = [cut(pltpu.roll(x, size - 1, axis)) for x in here]
                    bwd = [cut(pltpu.roll(x, 1, axis)) for x in here]
                    flux = add(mix(upw, d, fwd), mix(dnw, d, bwd))
                    acc = add(acc, [cs[d] * x for x in flux])
            new.append([inv * x for x in acc])
        delta = new
    for n in range(SW):
        for j in range(5):
            flow_out[j, n] = flow_out[j, n] + delta[n][j]

    for end in ends:
        end()


def per_device(spans, chords, *args):
    flow, node_dev = args[0], args[10].shape[1]
    layers, faces = flow.shape[1], args[8].shape[0] * args[8].shape[1]
    elems = args[14].shape[1]
    chunks = node_dev // LANES
    sems = 43 + 4 * (3 * chords - 1)
    tile = (ROWS, LANES)
    vmem = lambda *shape: pltpu.VMEM(shape, F32)
    span_edge, chord_edge = (SW, 5, layers, LANES), (SW, 5) + tile
    load = (chords, 3 * chunks, LANES)
    quantities = 4 * DEPTH
    table = ROWS * (chunks + 1)
    in_vmem = pl.BlockSpec(memory_space=pltpu.VMEM)
    in_smem = pl.BlockSpec(memory_space=pltpu.SMEM)
    specs = [in_vmem] * 4 + [in_smem] * 3 + [in_vmem] * 2 + [in_smem] + [in_vmem] * 5
    return pl.pallas_call(
        functools.partial(kernel, spans, chords),
        out_shape=(
            jax.ShapeDtypeStruct(flow.shape, F32),
            jax.ShapeDtypeStruct(args[10].shape, F32),
        ),
        in_specs=specs,
        out_specs=(in_vmem, in_vmem),
        scratch_shapes=[
            vmem(2, *flow.shape),
            vmem(*span_edge), vmem(*span_edge), vmem(*chord_edge), vmem(*chord_edge),
            vmem(*span_edge), vmem(*span_edge), vmem(*chord_edge), vmem(*chord_edge),
            vmem(*tile), vmem(*tile),
            vmem(chunks, 6, *tile), vmem(6, *tile),
            vmem(3, 3 * chunks, LANES), vmem(*load), vmem(*load), vmem(*load),
            vmem(4, *tile), vmem(2, 4, *tile),
            vmem(quantities, *tile), vmem(3, 3, quantities, *tile),
            vmem(SS, chords, table, LANES), vmem(SS, chords, *tile), vmem(SS, chords, *tile),
            vmem(*tile), vmem(*tile),
            vmem(3, *tile), vmem(5, 3, 3, *tile),
            pltpu.VMEM((3, LANES, faces), BF16),
            pltpu.VMEM((LANES, 4 * elems), BF16),
            vmem(3, 3, chunks, faces),
            pltpu.SemaphoreType.DMA((sems,)),
            pltpu.SemaphoreType.DMA((sems,)),
        ],
        compiler_params=pltpu.CompilerParams(
            collective_id=0, has_side_effects=True, vmem_limit_bytes=48 * 2**20
        ),
    )(*args)


def solution(mesh):
    spans, chords = mesh.shape["span"], mesh.shape["chord"]
    return jax.shard_map(
        functools.partial(per_device, spans, chords),
        mesh=mesh,
        in_specs=(
            P(None, None, "span", "chord"),
            P(None, None, "span", "chord"),
            P(None, "span", "chord"),
            P(None, None, "span", "chord"),
            P(),
            P(),
            P(),
            P(None, "span", "chord"),
            P("span", "chord"),
            P("span", "chord"),
            P(None, "span"),
            P(None, "span"),
            P(None, None, "span"),
            P(None, None, ("span", "chord")),
            P(None, ("span", "chord")),
        ),
        out_specs=(P(None, None, "span", "chord"), P(None, "span")),
        check_vma=False,
    )
```

```python
import functools

import jax
import jax.numpy as jnp
from jax import lax
from jax.experimental import pallas as pl
from jax.experimental.pallas import tpu as pltpu
from jax.sharding import PartitionSpec as P

SW = 4
SS = 3
LANES = 128
ROWS = 8
DEPTH = 3
MESH = pl.DeviceIdType.MESH
F32 = jnp.float32
BF16 = jnp.bfloat16


def split(x):
    lead = x.astype(BF16).astype(F32)
    return jnp.concatenate([lead, x - lead], axis=0).astype(BF16)


def halves(x):
    rows = x.shape[0] // 2
    return x[:rows] + x[rows:]


def dot_nn(a, b):
    return lax.dot_general(a, b, (((1,), (0,)), ((), ())), preferred_element_type=F32)


def dot_nt(a, b):
    return lax.dot_general(a, b, (((1,), (1,)), ((), ())), preferred_element_type=F32)


def flat(tile):
    return jnp.concatenate([tile[r : r + 1] for r in range(tile.shape[0])], axis=1)


def one_hot_lanes(low):
    rows = lax.broadcasted_iota(jnp.int32, (LANES, low.shape[1]), 0)
    return jnp.where(rows == low, 1.0, 0.0).astype(BF16)


def kernel(spans, chords, *refs):
    given, (flow_out, shell_out), local = refs[:15], refs[15:17], refs[17:32]
    in_sem, rest = refs[32], refs[33:]
    body(spans, chords, given, local, in_sem, flow_out, shell_out, *rest)


def body(
    spans, chords, given, local, in_sem, flow_out, shell_out, state, top_s, bot_s, lft_s, rgt_s, top_r, bot_r, lft_r, rgt_r,
    rim_s, rim_r, pt, ptrim, load_s, load_own, load_up, load_dn,
    face_s, face_r, ext_s, ext_r, kv, kv_prev, kv_next, rhs_s, rhs_r,
    ct, ct_r, hot_face, hot_elem, weight, send_sem, recv_sem,
):
    loading = [
        pltpu.make_async_copy(given[i], local[i], in_sem.at[i]) for i in range(len(given))
    ]
    for i in (0, 10, 9, 6, 7, 8, 14, 13, 11, 12, 3, 2, 1, 4, 5):
        loading[i].start()
    (flow, fgrad, diag, coup, upw, dnw, prow, fnorm, fnode, fcount, shell0, sgrad, precond,
     stiff, conn) = local

    def need(*which):
        for i in which:
            loading[i].wait()

    s = lax.axis_index("span")
    c = lax.axis_index("chord")
    layers = flow.shape[1]
    node_dev = shell0.shape[1]
    chunks = node_dev // LANES
    own_rows = ROWS * chunks
    has = {-1: s >= 1, 1: s < spans - 1, -2: s >= 2, 2: s < spans - 2, 0: None}
    hasc = {-1: c >= 1, 1: c < chords - 1, 0: None}

    def both(a, b):
        if a is None:
            return b
        return a if b is None else jnp.logical_and(a, b)

    def when(cond, run):
        if cond is None:
            run()
        else:
            pl.when(cond)(run)

    def mask(cond, x):
        return x if cond is None else jnp.where(cond, x, 0.0)

    barrier = pltpu.get_barrier_semaphore()
    expected = jnp.int32(0)
    for ds in range(-2, 3):
        for k in range(chords):
            if ds == 0 and k == 0:
                continue
            target = (s + ds, lax.rem(c + k, chords))
            when(
                has[ds],
                lambda target=target: pl.semaphore_signal(
                    barrier, inc=1, device_id=target, device_id_type=MESH
                ),
            )
            expected += 1 if ds == 0 else has[ds].astype(jnp.int32)

    ends = []
    used = [0]

    def transfer(src, dst, landing, target, goes, comes):
        i = used[0]
        used[0] += 1

        def make(where):
            return pltpu.make_async_remote_copy(
                src_ref=src, dst_ref=where, send_sem=send_sem.at[i],
                recv_sem=recv_sem.at[i], device_id=target, device_id_type=MESH,
            )

        when(goes, lambda: make(dst).start())
        ends.append(lambda: when(goes, lambda: make(dst).wait_send()))
        return lambda: when(comes, lambda: make(landing).wait_recv())

    def to_span(src, dst, ds):
        return transfer(src, dst, dst, (s + ds, c), has[ds], has[-ds])

    def to_chord(src, dst, dc):
        return transfer(src, dst, dst, (s, c + dc), hasc[dc], hasc[-dc])

    def to_all(src, buf, ds):
        out = []
        for k in range(1 if ds == 0 else 0, chords):
            target = (s + ds, lax.rem(c + k, chords))
            origin = lax.rem(c - k + chords, chords)
            out.append(
                transfer(src, buf.at[c], buf.at[origin], target, has[ds], has[-ds])
            )
        return out

    row = lax.broadcasted_iota(jnp.int32, (ROWS, LANES), 0)
    lane = lax.broadcasted_iota(jnp.int32, (ROWS, LANES), 1)
    zero = jnp.zeros((ROWS, LANES), F32)
    pad2 = jnp.zeros((2, LANES), F32)

    def chunk(ref, h):
        return jnp.concatenate([ref[:, h * LANES : (h + 1) * LANES], pad2], axis=0)

    need(10)
    field = jnp.concatenate([chunk(shell0, h) for h in range(chunks)], axis=0)
    rim_s[...] = field[:ROWS]

    def pack(tile, n, k, j, left, right):
        top_s[k, j, pl.ds(n, 1), :] = tile[0:1]
        bot_s[k, j, pl.ds(n, 1), :] = tile[ROWS - 1 : ROWS]
        left = jnp.where(lane == n, pltpu.roll(tile, n, 1), left)
        right = jnp.where(lane == n, pltpu.roll(tile, n + 1, 1), right)
        return left, right

    def store_packs(k, packs):
        for j in range(5):
            lft_s[k, j] = packs[2 * j]
            rgt_s[k, j] = packs[2 * j + 1]

    def first_edges(n, packs):
        out = []
        for j in range(5):
            out += pack(flow[j, n], n, 0, j, packs[2 * j], packs[2 * j + 1])
        return tuple(out)

    need(0)
    store_packs(0, lax.fori_loop(0, layers, first_edges, (zero,) * 10))

    pl.semaphore_wait(barrier, expected)

    rim_came = to_span(rim_s, rim_r, -1)

    def send_edges(k):
        return [
            to_span(top_s.at[k], top_r.at[k], -1),
            to_span(bot_s.at[k], bot_r.at[k], 1),
            to_chord(lft_s.at[k], lft_r.at[k], -1),
            to_chord(rgt_s.at[k], rgt_r.at[k], 1),
        ]

    edges_came = send_edges(0)

    need(9, 6, 7, 8)
    active = jnp.where(row * LANES + lane < fcount[0, 0], 1.0, 0.0)
    press = prow[0] * flow[0, 0]
    for j in range(1, 5):
        press = press + prow[j] * flow[j, 0]
    press = press * active
    nodes = flat(fnode[...])
    hot_face[1] = one_hot_lanes(jnp.bitwise_and(nodes, LANES - 1))
    own_chunk = jnp.right_shift(nodes - s * node_dev, 7)
    faces = nodes.shape[1]
    rows_f = lax.broadcasted_iota(jnp.int32, (chunks, faces), 0)
    loads = [flat(fnorm[i] * press) for i in range(3)]
    spread = []
    for owner in range(-1, 2):
        here = rows_f + owner * chunks == own_chunk
        for i in range(3):
            spread.append(jnp.where(here, loads[i], 0.0))
    partial = halves(dot_nt(split(jnp.concatenate(spread, axis=0)), hot_face[1]))
    third = 3 * chunks
    for o in range(3):
        load_s[o] = partial[o * third : (o + 1) * third]
    load_own[c] = partial[third : 2 * third]
    loads_came = to_all(load_s.at[1], load_own, 0)
    loads_came += to_all(load_s.at[2], load_up, 1)
    loads_came += to_all(load_s.at[0], load_dn, -1)

    need(14)
    enode = flat(conn[...] - s * node_dev)
    echunk = jnp.right_shift(enode, 7)
    hot_elem[...] = one_hot_lanes(jnp.bitwise_and(enode, LANES - 1))
    elems = conn.shape[1]

    def stiffness(field, rim, r):
        table = jnp.concatenate([field, rim], axis=0)
        got = halves(dot_nn(split(table), hot_elem[...]))
        u = jnp.where(echunk == 0, got[:ROWS], 0.0)
        for h in range(1, chunks + 1):
            u = jnp.where(echunk == h, got[h * ROWS : (h + 1) * ROWS], u)
        parts = [None] * 4
        for a in range(4):
            for d in range(6):
                term = stiff[6 * a + d] * u[d : d + 1, a * elems : (a + 1) * elems]
                parts[a] = term if parts[a] is None else parts[a] + term
        f = (parts[0] + parts[1]) + (parts[2] + parts[3])
        force = jnp.concatenate(
            [jnp.concatenate([f[6 * a : 6 * a + 6], pad2], axis=0) for a in range(4)], axis=1
        )
        spread = jnp.concatenate(
            [jnp.where(echunk == h, force, 0.0) for h in range(chunks + 1)], axis=0
        )
        kv[r, c] = halves(dot_nt(split(spread), hot_elem[...]))
        came = to_all(kv.at[r, c, pl.ds(own_rows, ROWS)], kv_prev.at[r], 1)
        if r < SS - 1:
            came += to_all(kv.at[r, c, pl.ds(0, ROWS)], kv_next.at[r], -1)
        return came + to_all(kv.at[r, c], kv.at[r], 0)

    rim_came()
    need(13)
    rim = mask(has[1], rim_r[...])
    kv_came = stiffness(field, rim, 0)

    need(12, 11)
    for d2 in range(6):
        col = jnp.concatenate(
            [precond[d, d2 : d2 + 1, :] for d in range(6)] + [jnp.zeros((2, node_dev), F32)], axis=0
        )
        for h in range(chunks):
            pt[h, d2] = col[:, h * LANES : (h + 1) * LANES]
    pt_came = to_span(pt.at[0], ptrim, -1)

    def total(buf):
        t = buf[0]
        for k in range(1, chords):
            t = t + buf[k]
        return t

    for came in loads_came:
        came()
    load = total(load_own) + mask(has[-1], total(load_up)) + mask(has[1], total(load_dn))
    rhs_rows = []
    for h in range(chunks):
        part = jnp.concatenate(
            [load[i * chunks + h : i * chunks + h + 1] for i in range(3)]
            + [jnp.zeros((ROWS - 3, LANES), F32)], axis=0,
        )
        rhs_rows.append(chunk(sgrad, h) - part)
    rhs = jnp.concatenate(rhs_rows, axis=0)
    rhs_s[...] = rhs[:ROWS]
    rhs_came = to_span(rhs_s, rhs_r, -1)

    need(3, 2, 1, 4, 5)
    node_f = fnode[...].astype(F32)
    for i in range(3):
        face_s[i] = fnorm[i] * active
    face_s[3] = node_f
    faces_came = [to_span(face_s, face_r.at[0], 1), to_span(face_s, face_r.at[1], -1)]
    for n in range(DEPTH):
        for k in range(3):
            ext_s[3 * n + k] = coup[k, n]
        ext_s[3 * DEPTH + n] = 1.0 / diag[n]
    ext_came = []
    for a in range(-1, 2):
        for b in range(-1, 2):
            if a == 0 and b == 0:
                continue
            slot = ext_r.at[a + 1, b + 1]
            ext_came.append(
                transfer(
                    ext_s, slot, slot, (s - a, c - b),
                    both(has[-a], hasc[-b]), both(has[a], hasc[b]),
                )
            )

    def mix(mat, k, tiles):
        out = []
        for i in range(5):
            t = mat[i, k, 0] * tiles[0]
            for j in range(1, 5):
                t = t + mat[i, k, j] * tiles[j]
            out.append(t)
        return out

    def flow_sweep(k, src, dst, came):
        for wait in came:
            wait()

        group = 2 if layers % 2 == 0 else 1

        def stack(tiles):
            return jnp.concatenate(tiles, axis=0)

        def around(d, j, n, cur):
            if d == 0:
                above, below = jnp.minimum(n + 1, layers - 1), jnp.maximum(n - 1, 0)
                return (
                    jnp.where(n < layers - 1, src(j, above), 0.0),
                    jnp.where(n > 0, src(j, below), 0.0),
                )
            if d == 1:
                down = mask(has[1], top_r[k, j, pl.ds(n, 1), :])
                up = mask(has[-1], bot_r[k, j, pl.ds(n, 1), :])
                return (
                    jnp.where(row == ROWS - 1, down, pltpu.roll(cur, ROWS - 1, 0)),
                    jnp.where(row == 0, up, pltpu.roll(cur, 1, 0)),
                )
            right = mask(hasc[1], pltpu.roll(lft_r[k, j], LANES - 1 - n, 1))
            left = mask(hasc[-1], pltpu.roll(rgt_r[k, j], LANES - n, 1))
            return (
                jnp.where(lane == LANES - 1, right, pltpu.roll(cur, LANES - 1, 1)),
                jnp.where(lane == 0, left, pltpu.roll(cur, 1, 1)),
            )

        def body(m, packs):
            ns = [group * m + g for g in range(group)]
            cur = [[src(j, n) for n in ns] for j in range(5)]
            acc = [stack([fgrad[j, n] for n in ns]) for j in range(5)]
            for d in range(3):
                pairs = [[around(d, j, n, cur[j][g]) for g, n in enumerate(ns)] for j in range(5)]
                fwd = [stack([p[0] for p in pair]) for pair in pairs]
                bwd = [stack([p[1] for p in pair]) for pair in pairs]
                one, two = mix(upw, d, fwd), mix(dnw, d, bwd)
                w = stack([coup[d, n] for n in ns])
                acc = [acc[i] + w * (one[i] + two[i]) for i in range(5)]
            inv = 1.0 / stack([diag[n] for n in ns])
            packs = list(packs)
            for j in range(5):
                both_tiles = inv * acc[j]
                for g, n in enumerate(ns):
                    tile = both_tiles[g * ROWS : (g + 1) * ROWS]
                    dst(j, n, tile)
                    if k < SW - 1:
                        packs[2 * j : 2 * j + 2] = pack(
                            tile, n, k + 1, j, packs[2 * j], packs[2 * j + 1]
                        )
            return tuple(packs)

        packs = lax.fori_loop(0, layers // group, body, (zero,) * 10 if k < SW - 1 else ())
        if k < SW - 1:
            store_packs(k + 1, packs)
            return send_edges(k + 1)
        return []

    def from_input(j, n):
        return flow[j, n]

    def reader(b):
        return lambda j, n: state[b, j, n]

    def writer(b):
        def put(j, n, tile):
            state[b, j, n] = tile

        return put

    def apply(blocks, res):
        out = blocks(0) * res[0:1]
        for d in range(1, 6):
            out = out + blocks(d) * res[d : d + 1]
        return out

    for r in range(SS):
        edges_came = flow_sweep(
            r, from_input if r == 0 else reader((r + 1) % 2), writer(r % 2), edges_came
        )
        if r == 0:
            for wait in faces_came:
                wait()
            for t in (-1, 0, 1):
                if t == 0:
                    tnodes, normals = nodes, [flat(face_s[i]) for i in range(3)]
                else:
                    got = face_r.at[0 if t == -1 else 1]
                    raw = mask(has[t], got[3]).astype(jnp.int32)
                    tnodes = flat(raw)
                    normals = [flat(mask(has[t], got[i])) for i in range(3)]
                    hot_face[t + 1] = one_hot_lanes(jnp.bitwise_and(tnodes, LANES - 1))
                here = rows_f == jnp.right_shift(tnodes - s * node_dev, 7)
                for i in range(3):
                    weight[t + 1, i] = jnp.where(here, normals[i], 0.0)
            pt_came()
            rhs_came()
            rhs_rim = mask(has[1], rhs_r[...])
        for wait in kv_came:
            wait()
        own = kv[r, 0, pl.ds(0, own_rows), :]
        for k in range(1, chords):
            own = own + kv[r, k, pl.ds(0, own_rows), :]
        spill = mask(has[-1], total(kv_prev.at[r]))
        res = rhs - jnp.concatenate([own[:ROWS] + spill, own[ROWS:]], axis=0)
        if r < SS - 1:
            mine = kv[r, 0, pl.ds(own_rows, ROWS), :]
            for k in range(1, chords):
                mine = mine + kv[r, k, pl.ds(own_rows, ROWS), :]
            res_rim = rhs_rim - (mask(has[1], total(kv_next.at[r])) + mine)
            rim = rim + mask(has[1], apply(lambda d: ptrim[d], res_rim))
        field = field + jnp.concatenate(
            [
                apply(lambda d, h=h: pt[h, d], res[h * ROWS : (h + 1) * ROWS])
                for h in range(chunks)
            ],
            axis=0,
        )
        if r < SS - 1:
            kv_came = stiffness(field, rim, r + 1)

    by_comp = jnp.concatenate(
        [field[h * ROWS + i : h * ROWS + i + 1] for i in range(3) for h in range(chunks)], axis=0
    )
    two = split(by_comp)
    for t in range(3):
        got = halves(dot_nn(two, hot_face[t]))
        acc = weight[t, 0] * got[:chunks]
        for i in range(1, 3):
            acc = acc + weight[t, i] * got[i * chunks : (i + 1) * chunks]
        share = jnp.sum(acc, axis=0, keepdims=True)
        ct[t] = jnp.concatenate(
            [share[:, r * LANES : (r + 1) * LANES] for r in range(ROWS)], axis=0
        )
    ct_came = []
    for ds in range(-2, 3):
        low, high = max(-1, ds - 1) + 1, min(1, ds + 1) + 2
        for dc in range(-1, 2):
            if ds == 0 and dc == 0:
                continue
            piece = pl.ds(low, high - low)
            slot = ct_r.at[2 - ds, 1 - dc, piece]
            ct_came.append(
                transfer(
                    ct.at[piece], slot, slot, (s + ds, c + dc),
                    both(has[ds], hasc[dc]), both(has[-ds], hasc[-dc]),
                )
            )
    for h in range(chunks):
        shell_out[:, h * LANES : (h + 1) * LANES] = field[h * ROWS : h * ROWS + 6]

    def put_out(j, n, tile):
        flow_out[j, n] = tile

    flow_sweep(SW - 1, reader((SW - 2) % 2), put_out, edges_came)

    for wait in ext_came:
        wait()

    def extended(get):
        def at(a, b):
            return get(a, b) if a == 0 and b == 0 else mask(both(has[a], hasc[b]), get(a, b))

        def sides(a):
            return jnp.where(lane < LANES // 2, at(a, 1), at(a, -1))

        upper = jnp.concatenate([at(0, 0), sides(0)], axis=1)
        span_halo = jnp.where(row < ROWS // 2, at(1, 0), at(-1, 0))
        corner = jnp.where(row < ROWS // 2, sides(1), sides(-1))
        return jnp.concatenate([upper, jnp.concatenate([span_halo, corner], axis=1)], axis=0)

    def ext_of(q):
        return extended(lambda a, b: ext_s[q] if a == 0 and b == 0 else ext_r[a + 1, b + 1, q])

    cext = [[ext_of(3 * n + k) for k in range(3)] for n in range(DEPTH)]
    iext = [ext_of(3 * DEPTH + n) for n in range(DEPTH)]

    for wait in ct_came:
        wait()

    def disp_at(tau, dc):
        out = None
        for t in range(-1, 2):
            sigma = tau - t
            if sigma == 0 and dc == 0:
                part = ct[t + 1]
            else:
                part = mask(both(has[sigma], hasc[dc]), ct_r[sigma + 2, dc + 1, t + 1])
            out = part if out is None else out + part
        return out

    disp = extended(disp_at)
    dsrc = [-prow[j] * disp for j in range(5)]

    def crop(x):
        return x[:ROWS, :LANES]

    def add(a, b):
        return b if a is None else [x + y for x, y in zip(a, b)]

    delta = [[iext[0] * dsrc[j] for j in range(5)]]
    for turn in range(1, SW):
        last = turn == SW - 1
        cut = crop if last else (lambda x: x)
        new = []
        for n in range(turn + 1):
            acc = [cut(x) for x in dsrc] if n == 0 else None
            if n < DEPTH:
                cs, inv = [cut(x) for x in cext[n]], cut(iext[n])
            else:
                cs, inv = [coup[k, n] for k in range(3)], 1.0 / diag[n]
            normal = None
            if n + 1 < len(delta):
                normal = mix(upw, 0, [cut(x) for x in delta[n + 1]])
            if n >= 1:
                normal = add(normal, mix(dnw, 0, [cut(x) for x in delta[n - 1]]))
            if normal is not None:
                acc = add(acc, [cs[0] * x for x in normal])
            if n < len(delta):
                here = delta[n]
                for d, axis, size in ((1, 0, 2 * ROWS), (2, 1, 2 * LANES)):
                    fwd = [cut(pltpu.roll(x, size - 1, axis)) for x in here]
                    bwd = [cut(pltpu.roll(x, 1, axis)) for x in here]
                    flux = add(mix(upw, d, fwd), mix(dnw, d, bwd))
                    acc = add(acc, [cs[d] * x for x in flux])
            new.append([inv * x for x in acc])
        delta = new
    for n in range(SW):
        for j in range(5):
            flow_out[j, n] = flow_out[j, n] + delta[n][j]

    for end in ends:
        end()


def hand_on(flow_in, shell_in, flow_out, shell_out, flow_v, shell_v, sem):
    parts = flow_in.shape[0]
    inward = [pltpu.make_async_copy(flow_in.at[j], flow_v.at[j], sem.at[0, j]) for j in range(parts)]
    inward.append(pltpu.make_async_copy(shell_in, shell_v, sem.at[0, parts]))
    out = [pltpu.make_async_copy(flow_v.at[j], flow_out.at[j], sem.at[1, j]) for j in range(parts)]
    out.append(pltpu.make_async_copy(shell_v, shell_out, sem.at[1, parts]))
    for copy in inward:
        copy.start()
    for one, two in zip(inward, out):
        one.wait()
        two.start()
    for copy in out:
        copy.wait()


def per_device(spans, chords, *args):
    turned = [jnp.transpose(args[i], (1, 0, 2)) for i in (4, 5)]
    args = args[:4] + tuple(turned) + args[6:]
    flow, node_dev = args[0], args[10].shape[1]
    layers, faces = flow.shape[1], args[8].shape[0] * args[8].shape[1]
    elems = args[14].shape[1]
    chunks = node_dev // LANES
    sems = 43 + 4 * (3 * chords - 1)
    tile = (ROWS, LANES)
    vmem = lambda *shape: pltpu.VMEM(shape, F32)
    span_edge, chord_edge = (SW, 5, layers, LANES), (SW, 5) + tile
    load = (chords, 3 * chunks, LANES)
    quantities = 4 * DEPTH
    table = ROWS * (chunks + 1)
    in_vmem = pl.BlockSpec(memory_space=pltpu.VMEM)
    in_hbm = pl.BlockSpec(memory_space=pltpu.HBM)
    scalars = (4, 5, 6, 9)
    kept = [
        (pltpu.SMEM if i in scalars else pltpu.VMEM)(a.shape, a.dtype) for i, a in enumerate(args)
    ]
    results = (
        jax.ShapeDtypeStruct(flow.shape, F32),
        jax.ShapeDtypeStruct(args[10].shape, F32),
    )
    made = pl.pallas_call(
        functools.partial(kernel, spans, chords),
        out_shape=results,
        in_specs=[in_hbm] * len(args),
        out_specs=(in_vmem, in_vmem),
        scratch_shapes=kept + [
            pltpu.SemaphoreType.DMA((len(args),)),
            vmem(2, *flow.shape),
            vmem(*span_edge), vmem(*span_edge), vmem(*chord_edge), vmem(*chord_edge),
            vmem(*span_edge), vmem(*span_edge), vmem(*chord_edge), vmem(*chord_edge),
            vmem(*tile), vmem(*tile),
            vmem(chunks, 6, *tile), vmem(6, *tile),
            vmem(3, 3 * chunks, LANES), vmem(*load), vmem(*load), vmem(*load),
            vmem(4, *tile), vmem(2, 4, *tile),
            vmem(quantities, *tile), vmem(3, 3, quantities, *tile),
            vmem(SS, chords, table, LANES), vmem(SS, chords, *tile), vmem(SS, chords, *tile),
            vmem(*tile), vmem(*tile),
            vmem(3, *tile), vmem(5, 3, 3, *tile),
            pltpu.VMEM((3, LANES, faces), BF16),
            pltpu.VMEM((LANES, 4 * elems), BF16),
            vmem(3, 3, chunks, faces),
            pltpu.SemaphoreType.DMA((sems,)),
            pltpu.SemaphoreType.DMA((sems,)),
        ],
        compiler_params=pltpu.CompilerParams(
            collective_id=0, has_side_effects=True, vmem_limit_bytes=63 * 2**20
        ),
    )(*args)
    return pl.pallas_call(
        hand_on,
        out_shape=results,
        in_specs=[in_hbm] * 2,
        out_specs=(in_hbm, in_hbm),
        scratch_shapes=[
            pltpu.VMEM(r.shape, F32) for r in results
        ] + [pltpu.SemaphoreType.DMA((2, flow.shape[0] + 1))],
        compiler_params=pltpu.CompilerParams(vmem_limit_bytes=63 * 2**20),
    )(*made)


def solution(mesh):
    spans, chords = mesh.shape["span"], mesh.shape["chord"]
    return jax.shard_map(
        functools.partial(per_device, spans, chords),
        mesh=mesh,
        in_specs=(
            P(None, None, "span", "chord"),
            P(None, None, "span", "chord"),
            P(None, "span", "chord"),
            P(None, None, "span", "chord"),
            P(),
            P(),
            P(),
            P(None, "span", "chord"),
            P("span", "chord"),
            P("span", "chord"),
            P(None, "span"),
            P(None, "span"),
            P(None, None, "span"),
            P(None, None, ("span", "chord")),
            P(None, ("span", "chord")),
        ),
        out_specs=(P(None, None, "span", "chord"), P(None, "span")),
        check_vma=False,
    )
```

```python
import functools

import jax
import jax.numpy as jnp
from jax import lax
from jax.experimental import pallas as pl
from jax.experimental.pallas import tpu as pltpu
from jax.sharding import PartitionSpec as P

SW = 4
SS = 3
LANES = 128
ROWS = 8
DEPTH = 3
MESH = pl.DeviceIdType.MESH
F32 = jnp.float32
BF16 = jnp.bfloat16


def split(x):
    lead = x.astype(BF16).astype(F32)
    return jnp.concatenate([lead, x - lead], axis=0).astype(BF16)


def halves(x):
    rows = x.shape[0] // 2
    return x[:rows] + x[rows:]


def dot_nn(a, b):
    return lax.dot_general(a, b, (((1,), (0,)), ((), ())), preferred_element_type=F32)


def dot_nt(a, b):
    return lax.dot_general(a, b, (((1,), (1,)), ((), ())), preferred_element_type=F32)


def flat(tile):
    return jnp.concatenate([tile[r : r + 1] for r in range(tile.shape[0])], axis=1)


def one_hot_lanes(low):
    rows = lax.broadcasted_iota(jnp.int32, (LANES, low.shape[1]), 0)
    return jnp.where(rows == low, 1.0, 0.0).astype(BF16)


def kernel(spans, chords, *refs):
    given, (flow_out, shell_out), local = refs[:15], refs[15:17], refs[17:32]
    in_sem, rest = refs[32], refs[33:]
    body(spans, chords, given, local, in_sem, flow_out, shell_out, *rest)


def body(
    spans, chords, given, local, in_sem, flow_out, shell_out, state, top_s, bot_s, lft_s, rgt_s, top_r, bot_r, lft_r, rgt_r,
    rim_s, rim_r, pt, ptrim, load_s, load_own, load_up, load_dn,
    face_s, face_r, ext_s, ext_r, kv, kv_prev, kv_next, rhs_s, rhs_r,
    ct, ct_r, hot_face, hot_elem, weight, send_sem, recv_sem,
):
    loading = [
        pltpu.make_async_copy(given[i], local[i], in_sem.at[i]) for i in range(len(given))
    ]
    for i in (0, 10, 9, 6, 7, 8, 14, 13, 11, 12, 3, 2, 1, 4, 5):
        loading[i].start()
    (flow, fgrad, diag, coup, upw, dnw, prow, fnorm, fnode, fcount, shell0, sgrad, precond,
     stiff, conn) = local

    def need(*which):
        for i in which:
            loading[i].wait()

    s = lax.axis_index("span")
    c = lax.axis_index("chord")
    layers = flow.shape[1]
    node_dev = shell0.shape[1]
    chunks = node_dev // LANES
    own_rows = ROWS * chunks
    has = {-1: s >= 1, 1: s < spans - 1, -2: s >= 2, 2: s < spans - 2, 0: None}
    hasc = {-1: c >= 1, 1: c < chords - 1, 0: None}

    def both(a, b):
        if a is None:
            return b
        return a if b is None else jnp.logical_and(a, b)

    def when(cond, run):
        if cond is None:
            run()
        else:
            pl.when(cond)(run)

    def mask(cond, x):
        return x if cond is None else jnp.where(cond, x, 0.0)

    barrier = pltpu.get_barrier_semaphore()
    expected = jnp.int32(0)
    for ds in range(-2, 3):
        for k in range(chords):
            if ds == 0 and k == 0:
                continue
            target = (s + ds, lax.rem(c + k, chords))
            when(
                has[ds],
                lambda target=target: pl.semaphore_signal(
                    barrier, inc=1, device_id=target, device_id_type=MESH
                ),
            )
            expected += 1 if ds == 0 else has[ds].astype(jnp.int32)

    ends = []
    used = [0]

    def transfer(src, dst, landing, target, goes, comes):
        i = used[0]
        used[0] += 1

        def make(where):
            return pltpu.make_async_remote_copy(
                src_ref=src, dst_ref=where, send_sem=send_sem.at[i],
                recv_sem=recv_sem.at[i], device_id=target, device_id_type=MESH,
            )

        when(goes, lambda: make(dst).start())
        ends.append(lambda: when(goes, lambda: make(dst).wait_send()))
        return lambda: when(comes, lambda: make(landing).wait_recv())

    def to_span(src, dst, ds):
        return transfer(src, dst, dst, (s + ds, c), has[ds], has[-ds])

    def to_chord(src, dst, dc):
        return transfer(src, dst, dst, (s, c + dc), hasc[dc], hasc[-dc])

    def to_all(src, buf, ds):
        out = []
        for k in range(1 if ds == 0 else 0, chords):
            target = (s + ds, lax.rem(c + k, chords))
            origin = lax.rem(c - k + chords, chords)
            out.append(
                transfer(src, buf.at[c], buf.at[origin], target, has[ds], has[-ds])
            )
        return out

    row = lax.broadcasted_iota(jnp.int32, (ROWS, LANES), 0)
    lane = lax.broadcasted_iota(jnp.int32, (ROWS, LANES), 1)
    zero = jnp.zeros((ROWS, LANES), F32)
    pad2 = jnp.zeros((2, LANES), F32)

    def chunk(ref, h):
        return jnp.concatenate([ref[:, h * LANES : (h + 1) * LANES], pad2], axis=0)

    need(10)
    field = jnp.concatenate([chunk(shell0, h) for h in range(chunks)], axis=0)
    rim_s[...] = field[:ROWS]

    def pack(tile, n, k, j, left, right):
        top_s[k, j, pl.ds(n, 1), :] = tile[0:1]
        bot_s[k, j, pl.ds(n, 1), :] = tile[ROWS - 1 : ROWS]
        left = jnp.where(lane == n, pltpu.roll(tile, n, 1), left)
        right = jnp.where(lane == n, pltpu.roll(tile, n + 1, 1), right)
        return left, right

    def store_packs(k, packs):
        for j in range(5):
            lft_s[k, j] = packs[2 * j]
            rgt_s[k, j] = packs[2 * j + 1]

    def first_edges(n, packs):
        out = []
        for j in range(5):
            out += pack(flow[j, n], n, 0, j, packs[2 * j], packs[2 * j + 1])
        return tuple(out)

    need(0)
    store_packs(0, lax.fori_loop(0, layers, first_edges, (zero,) * 10))

    pl.semaphore_wait(barrier, expected)

    rim_came = to_span(rim_s, rim_r, -1)

    def send_edges(k):
        return [
            to_span(top_s.at[k], top_r.at[k], -1),
            to_span(bot_s.at[k], bot_r.at[k], 1),
            to_chord(lft_s.at[k], lft_r.at[k], -1),
            to_chord(rgt_s.at[k], rgt_r.at[k], 1),
        ]

    edges_came = send_edges(0)

    need(9, 6, 7, 8)
    active = jnp.where(row * LANES + lane < fcount[0, 0], 1.0, 0.0)
    press = prow[0] * flow[0, 0]
    for j in range(1, 5):
        press = press + prow[j] * flow[j, 0]
    press = press * active
    nodes = flat(fnode[...])
    hot_face[1] = one_hot_lanes(jnp.bitwise_and(nodes, LANES - 1))
    own_chunk = jnp.right_shift(nodes - s * node_dev, 7)
    faces = nodes.shape[1]
    rows_f = lax.broadcasted_iota(jnp.int32, (chunks, faces), 0)
    loads = [flat(fnorm[i] * press) for i in range(3)]
    spread = []
    for owner in range(-1, 2):
        here = rows_f + owner * chunks == own_chunk
        for i in range(3):
            spread.append(jnp.where(here, loads[i], 0.0))
    partial = halves(dot_nt(split(jnp.concatenate(spread, axis=0)), hot_face[1]))
    third = 3 * chunks
    for o in range(3):
        load_s[o] = partial[o * third : (o + 1) * third]
    load_own[c] = partial[third : 2 * third]
    loads_came = to_all(load_s.at[1], load_own, 0)
    loads_came += to_all(load_s.at[2], load_up, 1)
    loads_came += to_all(load_s.at[0], load_dn, -1)

    need(14)
    enode = flat(conn[...] - s * node_dev)
    echunk = jnp.right_shift(enode, 7)
    hot_elem[...] = one_hot_lanes(jnp.bitwise_and(enode, LANES - 1))
    elems = conn.shape[1]

    def stiffness(field, rim, r):
        table = jnp.concatenate([field, rim], axis=0)
        got = halves(dot_nn(split(table), hot_elem[...]))
        u = jnp.where(echunk == 0, got[:ROWS], 0.0)
        for h in range(1, chunks + 1):
            u = jnp.where(echunk == h, got[h * ROWS : (h + 1) * ROWS], u)
        parts = [None] * 4
        for a in range(4):
            for d in range(6):
                term = stiff[6 * a + d] * u[d : d + 1, a * elems : (a + 1) * elems]
                parts[a] = term if parts[a] is None else parts[a] + term
        f = (parts[0] + parts[1]) + (parts[2] + parts[3])
        force = jnp.concatenate(
            [jnp.concatenate([f[6 * a : 6 * a + 6], pad2], axis=0) for a in range(4)], axis=1
        )
        spread = jnp.concatenate(
            [jnp.where(echunk == h, force, 0.0) for h in range(chunks + 1)], axis=0
        )
        kv[r, c] = halves(dot_nt(split(spread), hot_elem[...]))
        came = to_all(kv.at[r, c, pl.ds(own_rows, ROWS)], kv_prev.at[r], 1)
        if r < SS - 1:
            came += to_all(kv.at[r, c, pl.ds(0, ROWS)], kv_next.at[r], -1)
        return came + to_all(kv.at[r, c], kv.at[r], 0)

    rim_came()
    need(13)
    rim = mask(has[1], rim_r[...])
    kv_came = stiffness(field, rim, 0)

    need(12, 11)
    for d2 in range(6):
        col = jnp.concatenate(
            [precond[d, d2 : d2 + 1, :] for d in range(6)] + [jnp.zeros((2, node_dev), F32)], axis=0
        )
        for h in range(chunks):
            pt[h, d2] = col[:, h * LANES : (h + 1) * LANES]
    pt_came = to_span(pt.at[0], ptrim, -1)

    def total(buf):
        t = buf[0]
        for k in range(1, chords):
            t = t + buf[k]
        return t

    for came in loads_came:
        came()
    load = total(load_own) + mask(has[-1], total(load_up)) + mask(has[1], total(load_dn))
    rhs_rows = []
    for h in range(chunks):
        part = jnp.concatenate(
            [load[i * chunks + h : i * chunks + h + 1] for i in range(3)]
            + [jnp.zeros((ROWS - 3, LANES), F32)], axis=0,
        )
        rhs_rows.append(chunk(sgrad, h) - part)
    rhs = jnp.concatenate(rhs_rows, axis=0)
    rhs_s[...] = rhs[:ROWS]
    rhs_came = to_span(rhs_s, rhs_r, -1)

    need(3, 2, 1, 4, 5)
    node_f = fnode[...].astype(F32)
    for i in range(3):
        face_s[i] = fnorm[i] * active
    face_s[3] = node_f
    faces_came = [to_span(face_s, face_r.at[0], 1), to_span(face_s, face_r.at[1], -1)]
    for n in range(DEPTH):
        for k in range(3):
            ext_s[3 * n + k] = coup[k, n]
        ext_s[3 * DEPTH + n] = 1.0 / diag[n]
    ext_came = []
    for a in range(-1, 2):
        for b in range(-1, 2):
            if a == 0 and b == 0:
                continue
            slot = ext_r.at[a + 1, b + 1]
            ext_came.append(
                transfer(
                    ext_s, slot, slot, (s - a, c - b),
                    both(has[-a], hasc[-b]), both(has[a], hasc[b]),
                )
            )

    def mix(mat, k, tiles):
        out = []
        for i in range(5):
            t = mat[i, k, 0] * tiles[0]
            for j in range(1, 5):
                t = t + mat[i, k, j] * tiles[j]
            out.append(t)
        return out

    def flow_sweep(k, src, dst, came):
        for wait in came:
            wait()

        group = next(g for g in (4, 2, 1) if layers % g == 0)

        def stack(tiles):
            return jnp.concatenate(tiles, axis=0)

        def around(d, j, n, cur):
            if d == 0:
                above, below = jnp.minimum(n + 1, layers - 1), jnp.maximum(n - 1, 0)
                return (
                    jnp.where(n < layers - 1, src(j, above), 0.0),
                    jnp.where(n > 0, src(j, below), 0.0),
                )
            if d == 1:
                down = mask(has[1], top_r[k, j, pl.ds(n, 1), :])
                up = mask(has[-1], bot_r[k, j, pl.ds(n, 1), :])
                return (
                    jnp.where(row == ROWS - 1, down, pltpu.roll(cur, ROWS - 1, 0)),
                    jnp.where(row == 0, up, pltpu.roll(cur, 1, 0)),
                )
            right = mask(hasc[1], pltpu.roll(lft_r[k, j], LANES - 1 - n, 1))
            left = mask(hasc[-1], pltpu.roll(rgt_r[k, j], LANES - n, 1))
            return (
                jnp.where(lane == LANES - 1, right, pltpu.roll(cur, LANES - 1, 1)),
                jnp.where(lane == 0, left, pltpu.roll(cur, 1, 1)),
            )

        def body(m, packs):
            ns = [group * m + g for g in range(group)]
            cur = [[src(j, n) for n in ns] for j in range(5)]
            acc = [stack([fgrad[j, n] for n in ns]) for j in range(5)]
            for d in range(3):
                pairs = [[around(d, j, n, cur[j][g]) for g, n in enumerate(ns)] for j in range(5)]
                fwd = [stack([p[0] for p in pair]) for pair in pairs]
                bwd = [stack([p[1] for p in pair]) for pair in pairs]
                one, two = mix(upw, d, fwd), mix(dnw, d, bwd)
                w = stack([coup[d, n] for n in ns])
                acc = [acc[i] + w * (one[i] + two[i]) for i in range(5)]
            inv = 1.0 / stack([diag[n] for n in ns])
            packs = list(packs)
            for j in range(5):
                both_tiles = inv * acc[j]
                for g, n in enumerate(ns):
                    tile = both_tiles[g * ROWS : (g + 1) * ROWS]
                    dst(j, n, tile)
                    if k < SW - 1:
                        packs[2 * j : 2 * j + 2] = pack(
                            tile, n, k + 1, j, packs[2 * j], packs[2 * j + 1]
                        )
            return tuple(packs)

        packs = lax.fori_loop(0, layers // group, body, (zero,) * 10 if k < SW - 1 else ())
        if k < SW - 1:
            store_packs(k + 1, packs)
            return send_edges(k + 1)
        return []

    def from_input(j, n):
        return flow[j, n]

    def reader(b):
        return lambda j, n: state[b, j, n]

    def writer(b):
        def put(j, n, tile):
            state[b, j, n] = tile

        return put

    def apply(blocks, res):
        out = blocks(0) * res[0:1]
        for d in range(1, 6):
            out = out + blocks(d) * res[d : d + 1]
        return out

    for r in range(SS):
        edges_came = flow_sweep(
            r, from_input if r == 0 else reader((r + 1) % 2), writer(r % 2), edges_came
        )
        if r == 0:
            for wait in faces_came:
                wait()
            for t in (-1, 0, 1):
                if t == 0:
                    tnodes, normals = nodes, [flat(face_s[i]) for i in range(3)]
                else:
                    got = face_r.at[0 if t == -1 else 1]
                    raw = mask(has[t], got[3]).astype(jnp.int32)
                    tnodes = flat(raw)
                    normals = [flat(mask(has[t], got[i])) for i in range(3)]
                    hot_face[t + 1] = one_hot_lanes(jnp.bitwise_and(tnodes, LANES - 1))
                here = rows_f == jnp.right_shift(tnodes - s * node_dev, 7)
                for i in range(3):
                    weight[t + 1, i] = jnp.where(here, normals[i], 0.0)
            pt_came()
            rhs_came()
            rhs_rim = mask(has[1], rhs_r[...])
        for wait in kv_came:
            wait()
        own = kv[r, 0, pl.ds(0, own_rows), :]
        for k in range(1, chords):
            own = own + kv[r, k, pl.ds(0, own_rows), :]
        spill = mask(has[-1], total(kv_prev.at[r]))
        res = rhs - jnp.concatenate([own[:ROWS] + spill, own[ROWS:]], axis=0)
        if r < SS - 1:
            mine = kv[r, 0, pl.ds(own_rows, ROWS), :]
            for k in range(1, chords):
                mine = mine + kv[r, k, pl.ds(own_rows, ROWS), :]
            res_rim = rhs_rim - (mask(has[1], total(kv_next.at[r])) + mine)
            rim = rim + mask(has[1], apply(lambda d: ptrim[d], res_rim))
        field = field + jnp.concatenate(
            [
                apply(lambda d, h=h: pt[h, d], res[h * ROWS : (h + 1) * ROWS])
                for h in range(chunks)
            ],
            axis=0,
        )
        if r < SS - 1:
            kv_came = stiffness(field, rim, r + 1)

    by_comp = jnp.concatenate(
        [field[h * ROWS + i : h * ROWS + i + 1] for i in range(3) for h in range(chunks)], axis=0
    )
    two = split(by_comp)
    for t in range(3):
        got = halves(dot_nn(two, hot_face[t]))
        acc = weight[t, 0] * got[:chunks]
        for i in range(1, 3):
            acc = acc + weight[t, i] * got[i * chunks : (i + 1) * chunks]
        share = jnp.sum(acc, axis=0, keepdims=True)
        ct[t] = jnp.concatenate(
            [share[:, r * LANES : (r + 1) * LANES] for r in range(ROWS)], axis=0
        )
    ct_came = []
    for ds in range(-2, 3):
        low, high = max(-1, ds - 1) + 1, min(1, ds + 1) + 2
        for dc in range(-1, 2):
            if ds == 0 and dc == 0:
                continue
            piece = pl.ds(low, high - low)
            slot = ct_r.at[2 - ds, 1 - dc, piece]
            ct_came.append(
                transfer(
                    ct.at[piece], slot, slot, (s + ds, c + dc),
                    both(has[ds], hasc[dc]), both(has[-ds], hasc[-dc]),
                )
            )
    for h in range(chunks):
        shell_out[:, h * LANES : (h + 1) * LANES] = field[h * ROWS : h * ROWS + 6]

    def put_out(j, n, tile):
        flow_out[j, n] = tile

    flow_sweep(SW - 1, reader((SW - 2) % 2), put_out, edges_came)

    for wait in ext_came:
        wait()

    def extended(get):
        def at(a, b):
            return get(a, b) if a == 0 and b == 0 else mask(both(has[a], hasc[b]), get(a, b))

        def sides(a):
            return jnp.where(lane < LANES // 2, at(a, 1), at(a, -1))

        upper = jnp.concatenate([at(0, 0), sides(0)], axis=1)
        span_halo = jnp.where(row < ROWS // 2, at(1, 0), at(-1, 0))
        corner = jnp.where(row < ROWS // 2, sides(1), sides(-1))
        return jnp.concatenate([upper, jnp.concatenate([span_halo, corner], axis=1)], axis=0)

    def ext_of(q):
        return extended(lambda a, b: ext_s[q] if a == 0 and b == 0 else ext_r[a + 1, b + 1, q])

    cext = [[ext_of(3 * n + k) for k in range(3)] for n in range(DEPTH)]
    iext = [ext_of(3 * DEPTH + n) for n in range(DEPTH)]

    for wait in ct_came:
        wait()

    def disp_at(tau, dc):
        out = None
        for t in range(-1, 2):
            sigma = tau - t
            if sigma == 0 and dc == 0:
                part = ct[t + 1]
            else:
                part = mask(both(has[sigma], hasc[dc]), ct_r[sigma + 2, dc + 1, t + 1])
            out = part if out is None else out + part
        return out

    disp = extended(disp_at)
    dsrc = [-prow[j] * disp for j in range(5)]

    def crop(x):
        return x[:ROWS, :LANES]

    def add(a, b):
        return b if a is None else [x + y for x, y in zip(a, b)]

    delta = [[iext[0] * dsrc[j] for j in range(5)]]
    for turn in range(1, SW):
        last = turn == SW - 1
        cut = crop if last else (lambda x: x)
        new = []
        for n in range(turn + 1):
            acc = [cut(x) for x in dsrc] if n == 0 else None
            if n < DEPTH:
                cs, inv = [cut(x) for x in cext[n]], cut(iext[n])
            else:
                cs, inv = [coup[k, n] for k in range(3)], 1.0 / diag[n]
            normal = None
            if n + 1 < len(delta):
                normal = mix(upw, 0, [cut(x) for x in delta[n + 1]])
            if n >= 1:
                normal = add(normal, mix(dnw, 0, [cut(x) for x in delta[n - 1]]))
            if normal is not None:
                acc = add(acc, [cs[0] * x for x in normal])
            if n < len(delta):
                here = delta[n]
                for d, axis, size in ((1, 0, 2 * ROWS), (2, 1, 2 * LANES)):
                    fwd = [cut(pltpu.roll(x, size - 1, axis)) for x in here]
                    bwd = [cut(pltpu.roll(x, 1, axis)) for x in here]
                    flux = add(mix(upw, d, fwd), mix(dnw, d, bwd))
                    acc = add(acc, [cs[d] * x for x in flux])
            new.append([inv * x for x in acc])
        delta = new
    for n in range(SW):
        for j in range(5):
            flow_out[j, n] = flow_out[j, n] + delta[n][j]

    for end in ends:
        end()


def hand_on(flow_in, shell_in, flow_out, shell_out, flow_v, shell_v, sem):
    parts = flow_in.shape[0]
    inward = [pltpu.make_async_copy(flow_in.at[j], flow_v.at[j], sem.at[0, j]) for j in range(parts)]
    inward.append(pltpu.make_async_copy(shell_in, shell_v, sem.at[0, parts]))
    out = [pltpu.make_async_copy(flow_v.at[j], flow_out.at[j], sem.at[1, j]) for j in range(parts)]
    out.append(pltpu.make_async_copy(shell_v, shell_out, sem.at[1, parts]))
    for copy in inward:
        copy.start()
    for one, two in zip(inward, out):
        one.wait()
        two.start()
    for copy in out:
        copy.wait()


def per_device(spans, chords, *args):
    turned = [jnp.transpose(args[i], (1, 0, 2)) for i in (4, 5)]
    args = args[:4] + tuple(turned) + args[6:]
    flow, node_dev = args[0], args[10].shape[1]
    layers, faces = flow.shape[1], args[8].shape[0] * args[8].shape[1]
    elems = args[14].shape[1]
    chunks = node_dev // LANES
    sems = 43 + 4 * (3 * chords - 1)
    tile = (ROWS, LANES)
    vmem = lambda *shape: pltpu.VMEM(shape, F32)
    span_edge, chord_edge = (SW, 5, layers, LANES), (SW, 5) + tile
    load = (chords, 3 * chunks, LANES)
    quantities = 4 * DEPTH
    table = ROWS * (chunks + 1)
    in_vmem = pl.BlockSpec(memory_space=pltpu.VMEM)
    in_hbm = pl.BlockSpec(memory_space=pltpu.HBM)
    scalars = (4, 5, 6, 9)
    kept = [
        (pltpu.SMEM if i in scalars else pltpu.VMEM)(a.shape, a.dtype) for i, a in enumerate(args)
    ]
    results = (
        jax.ShapeDtypeStruct(flow.shape, F32),
        jax.ShapeDtypeStruct(args[10].shape, F32),
    )
    made = pl.pallas_call(
        functools.partial(kernel, spans, chords),
        out_shape=results,
        in_specs=[in_hbm] * len(args),
        out_specs=(in_vmem, in_vmem),
        scratch_shapes=kept + [
            pltpu.SemaphoreType.DMA((len(args),)),
            vmem(2, *flow.shape),
            vmem(*span_edge), vmem(*span_edge), vmem(*chord_edge), vmem(*chord_edge),
            vmem(*span_edge), vmem(*span_edge), vmem(*chord_edge), vmem(*chord_edge),
            vmem(*tile), vmem(*tile),
            vmem(chunks, 6, *tile), vmem(6, *tile),
            vmem(3, 3 * chunks, LANES), vmem(*load), vmem(*load), vmem(*load),
            vmem(4, *tile), vmem(2, 4, *tile),
            vmem(quantities, *tile), vmem(3, 3, quantities, *tile),
            vmem(SS, chords, table, LANES), vmem(SS, chords, *tile), vmem(SS, chords, *tile),
            vmem(*tile), vmem(*tile),
            vmem(3, *tile), vmem(5, 3, 3, *tile),
            pltpu.VMEM((3, LANES, faces), BF16),
            pltpu.VMEM((LANES, 4 * elems), BF16),
            vmem(3, 3, chunks, faces),
            pltpu.SemaphoreType.DMA((sems,)),
            pltpu.SemaphoreType.DMA((sems,)),
        ],
        compiler_params=pltpu.CompilerParams(
            collective_id=0, has_side_effects=True, vmem_limit_bytes=63 * 2**20
        ),
    )(*args)
    return pl.pallas_call(
        hand_on,
        out_shape=results,
        in_specs=[in_hbm] * 2,
        out_specs=(in_hbm, in_hbm),
        scratch_shapes=[
            pltpu.VMEM(r.shape, F32) for r in results
        ] + [pltpu.SemaphoreType.DMA((2, flow.shape[0] + 1))],
        compiler_params=pltpu.CompilerParams(vmem_limit_bytes=63 * 2**20),
    )(*made)


def solution(mesh):
    spans, chords = mesh.shape["span"], mesh.shape["chord"]
    return jax.shard_map(
        functools.partial(per_device, spans, chords),
        mesh=mesh,
        in_specs=(
            P(None, None, "span", "chord"),
            P(None, None, "span", "chord"),
            P(None, "span", "chord"),
            P(None, None, "span", "chord"),
            P(),
            P(),
            P(),
            P(None, "span", "chord"),
            P("span", "chord"),
            P("span", "chord"),
            P(None, "span"),
            P(None, "span"),
            P(None, None, "span"),
            P(None, None, ("span", "chord")),
            P(None, ("span", "chord")),
        ),
        out_specs=(P(None, None, "span", "chord"), P(None, "span")),
        check_vma=False,
    )
```
